32 devices in a mesh: expert: 8 (over z, core), blk: 4 (over y, x).
Axes of the slice: x: 2, y: 2, z: 4, core: 2. Of those that a mesh axis runs over, the one named last changes fastest.
Arguments:
- tokens: bfloat16 [4096, 3584], P('expert', 'blk'), may hold values from -6 to 6
- route: int32 [4096, 1], P('expert'), may hold values from 0 to 7; in each aligned block of 512 rows (0 to 511, 512 to 1023, ...) at most 96 rows name the same one
- gate_score: float32 [4096, 1], P('expert'), may hold values from 0.1 to 1
- w_gate: bfloat16 [8, 3584, 2048], P('expert', None, 'blk'), may hold values from -0.09375 to 0.09375
- w_up: bfloat16 [8, 3584, 2048], P('expert', None, 'blk'), may hold values from -0.09375 to 0.09375
- w_down: bfloat16 [8, 2048, 3584], P('expert', 'blk'), may hold values from -0.125 to 0.125
Outputs:
- mixed: bfloat16 [4096, 3584], P('expert', 'blk')
The draws below stay inside these ranges and needn't reach their ends.
Inputs may be any that keep to these rules, and one draw needn't show every extreme that they name: `route`: among the 512 tokens of one index of expert (aligned blocks of rows), no expert is named more than 96 times, a bound that some block reaches.
All inputs are finite; a program needn't handle non-finite values.
Results may differ from the reference program's by a relative error of at most 0.015.
Values may be sent and summed in bfloat16 or wider, within the bound.
No kernel may reach another device: no remote copies, remote signals or barrier semaphores. Data moves between devices by JAX's collectives and lax.ppermute only.
A program may use at most 64 MiB of HBM per device.

```python
import math
import jax
import jax.numpy as jnp
import numpy as np
from jax import lax

D = 3584
FF = 2048
TOK_DEV = 512
EXPERTS = 8
CAP = 96
TOKENS = 4096
N_BLK = 4


def steps_of(own_key, shape, split, smallest, high):
    level, own = 1.0, jax.random.fold_in(own_key, 6)
    for dim, shards_of in split:
        steps = jnp.exp(jax.random.uniform(jax.random.fold_in(own, dim), (shards_of,), jnp.float32, smallest / len(split), high / len(split)))
        level = level * jnp.repeat(steps, shape[dim] // shards_of).reshape([-1 if axis == dim else 1 for axis in range(len(shape))])
    return level


def assign_block(own_key, own, number, rows, count, top, bound, skew):
    order = jax.random.permutation(own_key, count)
    heavy_load, usual = portions_of(count, rows * top, bound, skew, True), portions_of(count, rows * top, bound, skew, False)
    places = jnp.arange(count)

    def named(tallies, offset_by):
        used = int((tallies > 0).sum())
        fixed = max(1, used // 4)
        passed = fixed + (places - fixed + offset_by * (used - fixed)) % max(1, count - fixed)
        return jnp.zeros((count,), jnp.int32).at[order[jnp.where(places < fixed, places, passed)]].set(jnp.asarray(tallies, jnp.int32))

    tallies = jnp.where(number % 4 == 0, named(heavy_load, number // 4), named(usual, number - number // 4 - 1))
    mixed = jax.random.permutation(jax.random.fold_in(own, 3), count)
    giver, receiver = mixed[0:count // 2 * 2:2], mixed[1:count // 2 * 2:2]
    room = jnp.minimum(tallies[giver] - 1, bound - tallies[receiver]) // 2
    room = jnp.where((giver == order[0]) | (receiver == order[0]) | (tallies[receiver] == 0), 0, jnp.maximum(room, 0))
    passed = jax.random.randint(jax.random.fold_in(own, 4), (count // 2,), 0, 1 << 20) % (room + 1)
    tallies = tallies.at[giver].add(-passed).at[receiver].add(passed)
    items = jnp.searchsorted(jnp.cumsum(tallies), jnp.arange(rows * top), side="right").astype(jnp.int32)
    table = items.reshape(top, rows).T
    table = table[jax.random.permutation(jax.random.fold_in(own, 1), rows)]
    offset_by = jax.random.randint(jax.random.fold_in(own, 2), (rows, 1), 0, top)
    return jnp.take_along_axis(table, (jnp.arange(top)[None, :] + offset_by) % top, axis=1)


def portions_of(number_of, total, limit, skew, full):
    portions = [(1 << 20) // math.isqrt(grade ** skew) + 1 for grade in range(1, number_of + 1)]
    largest = limit if full else min(limit, max(-(-total // number_of), total * portions[0] // sum(portions)))
    least = 1 if total - largest >= number_of - 1 else 0
    given, rest = [largest] + [least] * (number_of - 1), total - largest - least * (number_of - 1)
    while rest > 0:
        movable = [i for i in range(1, number_of) if given[i] < largest] or [i for i in range(1, number_of) if given[i] < limit]
        whole, remaining = sum([portions[i] for i in movable]), rest
        for i in movable:
            more = min(limit - given[i], max(1, remaining * portions[i] // whole), rest)
            given[i] = given[i] + more
            rest = rest - more
    return np.array(given)


def noise(key, dims, scale, bound, cuts=(), kind=jnp.bfloat16):
    drawn = scale * jax.random.normal(key, dims, jnp.float32)
    if cuts:
        drawn = drawn * steps_of(key, dims, cuts, -0.22, 0.18)
    return jnp.clip(drawn, -bound, bound).astype(kind)


def setup_inputs(seed: int = 0) -> dict:
    key_list = jax.random.split(jax.random.key(seed), 7)
    tokens = noise(key_list[0], (TOKENS, D), 1.0, 6.0, ((0, 8), (1, 4)))
    route_keys = jax.random.split(jax.random.fold_in(key_list[1], 1), TOKENS // TOK_DEV)
    route_turns = jax.random.permutation(jax.random.fold_in(key_list[1], 3), TOKENS // TOK_DEV)
    route = jax.vmap(lambda own, number: assign_block(jax.random.fold_in(key_list[1], 2), own, number, TOK_DEV, EXPERTS, 1, CAP, 2))(route_keys, route_turns).reshape((TOKENS, 1))
    gate_score = jnp.clip(jnp.exp(math.log(1.0) - 2.3025851 * jax.random.uniform(key_list[2], (TOKENS, 1), jnp.float32) ** steps_of(key_list[2], (TOKENS, 1), ((0, 8),), -0.2, 0.2)), 0.1, 1.0)
    w_gate = noise(key_list[3], (EXPERTS, D, FF), D ** -0.5, 0.09375, ((0, 8), (2, 4)))
    w_up = noise(key_list[4], (EXPERTS, D, FF), D ** -0.5, 0.09375, ((0, 8), (2, 4)))
    w_down = noise(key_list[5], (EXPERTS, FF, D), FF ** -0.5, 0.125, ((0, 8), (1, 4)))
    return dict(tokens=tokens, route=route, gate_score=gate_score, w_gate=w_gate, w_up=w_up, w_down=w_down)


def reference(tokens, route, gate_score, w_gate, w_up, w_down):
    total = tokens.shape[0]
    blocks = total // TOK_DEV
    target = route[:, 0].astype(jnp.int32)
    grid = target.reshape(blocks, TOK_DEV)
    onehot = (grid[:, :, None] == jnp.arange(EXPERTS, dtype=jnp.int32)[None, None, :]).astype(jnp.int32)
    earlier = jnp.cumsum(onehot, axis=1) - onehot
    rank = jnp.sum(earlier * onehot, axis=2).reshape(total).astype(jnp.int32)
    block_id = (jnp.arange(total, dtype=jnp.int32) // TOK_DEV).astype(jnp.int32)
    slot = (block_id * CAP + rank).astype(jnp.int32)
    table = jnp.zeros((EXPERTS, blocks * CAP), jnp.int32).at[target, slot].set(jnp.arange(total, dtype=jnp.int32))
    filled = jnp.zeros((EXPERTS, blocks * CAP), jnp.float32).at[target, slot].set(1.0)
    width = FF // N_BLK

    def run_expert(index):
        rows = tokens[table[index]] * filled[index][:, None].astype(jnp.bfloat16)
        gate = jnp.dot(rows, w_gate[index], preferred_element_type=jnp.float32)
        up = jnp.dot(rows, w_up[index], preferred_element_type=jnp.float32)
        hidden = (jax.nn.silu(gate) * up).astype(jnp.bfloat16)
        parts = jnp.einsum("sbf,bfd->bsd", hidden.reshape(-1, N_BLK, width).astype(jnp.float32), w_down[index].reshape(N_BLK, width, D).astype(jnp.float32))
        rounded = lax.optimization_barrier(parts.astype(jnp.bfloat16))
        return jnp.sum(rounded.astype(jnp.float32), axis=0).astype(jnp.bfloat16)

    outputs = lax.map(run_expert, jnp.arange(EXPERTS, dtype=jnp.int32))
    expert_out = outputs[target, slot]
    return (expert_out.astype(jnp.float32) * gate_score).astype(jnp.bfloat16)
```

```python
import functools
import jax
import jax.numpy as jnp
from jax import lax
from jax.experimental import pallas as pl
from jax.experimental.pallas import tpu as pltpu
from jax.sharding import PartitionSpec as P


def slot_ids_of(route):
    count = route.shape[0]
    target = route[:, 0]
    later = lax.broadcasted_iota(jnp.int32, (count, count), 0)
    before = lax.broadcasted_iota(jnp.int32, (count, count), 1) < later
    same = target[:, None] == target[None, :]
    rank = jnp.sum(jnp.where(same & before, 1, 0), axis=1).astype(jnp.int32)
    return target, rank


def selector_of(target, rank, groups, first, slots):
    inside = (rank >= first) & (rank < first + slots)
    ids = jnp.where(inside, target * slots + rank - first, -1)
    positions = lax.broadcasted_iota(jnp.int32, (groups * slots, target.shape[0]), 0)
    return (positions == ids[None, :]).astype(jnp.bfloat16)


def ffn_kernel(me, x0, x1, x2, x3a, x3b, wg, wu, wd, p0, p1, p2, p3a, p3b, gate, up, hidden):
    step = pl.program_id(0)
    half = x3a.shape[0]

    def add(rows, x, first):
        g = jnp.dot(x[...], wg[0], preferred_element_type=jnp.float32)
        u = jnp.dot(x[...], wu[0], preferred_element_type=jnp.float32)
        if first:
            gate[rows, :] = g
            up[rows, :] = u
        else:
            gate[rows, :] += g
            up[rows, :] += u

    whole, top, bottom = slice(None), slice(0, half), slice(half, None)

    @pl.when(step == 0)
    def _():
        add(whole, x0, True)

    @pl.when(step == 1)
    def _():
        add(whole, x1, False)

    @pl.when(step == 2)
    def _():
        add(whole, x2, False)

    @pl.when(step == 3)
    def _():
        add(top, x3a, False)
        add(bottom, x3b, False)
        v = gate[...]
        hidden[...] = (v / (1.0 + jnp.exp(-v)) * up[...]).astype(jnp.bfloat16)

    def part():
        return jnp.dot(hidden[...], wd[...], preferred_element_type=jnp.float32).astype(jnp.bfloat16)

    @pl.when(step == 4)
    def _():
        p = part()
        p3a[...] = p[:half]
        p3b[...] = p[half:]

    @pl.when(step == 5)
    def _():
        p2[...] = part()

    @pl.when(step == 6)
    def _():
        p1[...] = part()

    @pl.when(step == 7)
    def _():
        p0[...] = part()


def ffn(me, x0, x1, x2, x3a, x3b, wg, wu, wd):
    rows, width = x0.shape
    half = rows // 2
    hid = wg.shape[-1]
    n = wg.shape[0]
    full = lambda r: pl.BlockSpec((r, width), lambda j, me: (0, 0))
    w_in = pl.BlockSpec((1, width, hid), lambda j, me: (me[0] ^ jnp.minimum(j, n - 1), 0, 0))
    w_out = pl.BlockSpec((hid, width), lambda j, me: (0, me[0] ^ (2 * n - 1 - jnp.maximum(j, n))))
    sds = lambda r: jax.ShapeDtypeStruct((r, width), jnp.bfloat16)
    return pl.pallas_call(
        ffn_kernel,
        grid_spec=pltpu.PrefetchScalarGridSpec(
            num_scalar_prefetch=1,
            grid=(2 * n,),
            in_specs=[full(rows)] * 3 + [full(half)] * 2 + [w_in, w_in, w_out],
            out_specs=[full(rows)] * 3 + [full(half)] * 2,
            scratch_shapes=[
                pltpu.VMEM((rows, hid), jnp.float32),
                pltpu.VMEM((rows, hid), jnp.float32),
                pltpu.VMEM((rows, hid), jnp.bfloat16),
            ],
        ),
        out_shape=[sds(rows)] * 3 + [sds(half)] * 2,
        compiler_params=pltpu.CompilerParams(vmem_limit_bytes=40 * 1024 * 1024),
        cost_estimate=pl.CostEstimate(
            flops=6 * rows * n * width * hid, bytes_accessed=6 * n * width * hid, transcendentals=rows * hid
        ),
    )(me, x0, x1, x2, x3a, x3b, wg, wu, wd)


def square_layer(arrived, me, wg, wu, wd):
    to_x = [(i, i ^ 1) for i in range(4)]
    to_y = [(i, i ^ 2) for i in range(4)]
    send = lambda a, to: lax.ppermute(a, "blk", to)
    half = arrived.shape[0] // 2
    x1 = send(arrived, to_x)
    x2 = send(arrived, to_y)
    x3a = send(x2[:half], to_x)
    x3b = send(x1[half:], to_y)
    p0, p1, p2, p3a, p3b = ffn(me, arrived, x1, x2, x3a, x3b, wg, wu, wd)
    f32 = lambda a: a.astype(jnp.float32)
    q2a = send(p3a, to_x)
    q1b = send(p3b, to_y)
    p1 = jnp.concatenate([p1[:half], (f32(p1[half:]) + f32(q1b)).astype(jnp.bfloat16)], 0)
    p2 = jnp.concatenate([(f32(p2[:half]) + f32(q2a)).astype(jnp.bfloat16), p2[half:]], 0)
    q0 = send(p1, to_x)
    r0 = send(p2, to_y)
    return (f32(p0) + f32(q0) + f32(r0)).astype(jnp.bfloat16)


def plain_layer(arrived, w_gate, w_up, w_down):
    whole = lax.all_gather(arrived, "blk", axis=1, tiled=True)
    gate_acc = jnp.dot(whole, w_gate, preferred_element_type=jnp.float32)
    up_acc = jnp.dot(whole, w_up, preferred_element_type=jnp.float32)
    hidden = (jax.nn.silu(gate_acc) * up_acc).astype(jnp.bfloat16)
    partial_sum = jnp.dot(hidden, w_down, preferred_element_type=jnp.float32)
    return lax.psum_scatter(partial_sum.astype(jnp.bfloat16), "blk", scatter_dimension=1, tiled=True)


CHUNKS = (1, 1, 1)


def per_device(tokens, route, gate_score, w_gate, w_up, w_down):
    groups = lax.axis_size("expert")
    n = lax.axis_size("blk")
    count, width = tokens.shape
    capacity = 3 * count // (2 * groups)
    target, rank = slot_ids_of(route)
    square = n == 4 and width % 128 == 0
    wg, wu, wd = w_gate[0], w_up[0], w_down[0]
    if square:
        me = lax.axis_index("blk").astype(jnp.int32).reshape(1)
        wg, wu = wg.reshape(n, width, -1), wu.reshape(n, width, -1)
    exchange = lambda a: lax.all_to_all(a, "expert", split_axis=0, concat_axis=0, tiled=True)
    unit = capacity // sum(CHUNKS)
    first, total = 0, None
    for part in CHUNKS:
        slots = unit * part
        selector = selector_of(target, rank, groups, first, slots)
        first += slots
        outgoing = jnp.dot(selector, tokens, preferred_element_type=jnp.float32).astype(jnp.bfloat16)
        arrived = exchange(outgoing)
        shares = square_layer(arrived, me, wg, wu, wd) if square else plain_layer(arrived, wg, wu, wd)
        back = exchange(shares)
        picked = lax.dot_general(selector, back, (((0,), (0,)), ((), ())), preferred_element_type=jnp.float32)
        total = picked if total is None else total + picked
    return (total * gate_score).astype(jnp.bfloat16)


def solution(mesh):
    in_specs = (
        P("expert", "blk"),
        P("expert", None),
        P("expert", None),
        P("expert", None, "blk"),
        P("expert", None, "blk"),
        P("expert", "blk", None),
    )
    return jax.shard_map(
        per_device, mesh=mesh, in_specs=in_specs, out_specs=P("expert", "blk"), check_vma=False
    )
```

```python
import jax
import jax.numpy as jnp
from jax import lax
from jax.experimental import pallas as pl
from jax.experimental.pallas import tpu as pltpu
from jax.sharding import PartitionSpec as P

RING = (0, 1, 3, 2)


def rank_of(target):
    count = target.shape[0]
    later = lax.broadcasted_iota(jnp.int32, (count, count), 0)
    before = lax.broadcasted_iota(jnp.int32, (count, count), 1) < later
    same = target[:, None] == target[None, :]
    return jnp.sum(jnp.where(same & before, 1, 0), axis=1).astype(jnp.int32)


def selector_of(slot_ids, slots):
    positions = lax.broadcasted_iota(jnp.int32, (slots, slot_ids.shape[0]), 0)
    return (positions == slot_ids[None, :]).astype(jnp.bfloat16)


def hidden_kernel(order, x0, x1, x2, x3, wg, wu, wd, hidden, part):
    width = x0.shape[1]
    gate = up = None
    for j, x in enumerate((x0, x1, x2, x3)):
        rows = pl.ds(pl.multiple_of(order[j] * width, width), width)
        g = jnp.dot(x[...], wg[rows, :], preferred_element_type=jnp.float32)
        u = jnp.dot(x[...], wu[rows, :], preferred_element_type=jnp.float32)
        gate, up = (g, u) if gate is None else (gate + g, up + u)
    hidden[...] = (gate / (1.0 + jnp.exp(-gate)) * up).astype(jnp.bfloat16)
    cols = pl.ds(pl.multiple_of(order[1] * width, width), width)
    part[...] = jnp.dot(hidden[...], wd[:, cols], preferred_element_type=jnp.float32).astype(jnp.bfloat16)


def down_kernel(j, order, hidden, arrived, wd, out):
    width = out.shape[1]
    cols = pl.ds(pl.multiple_of(order[j] * width, width), width)
    part = jnp.dot(hidden[...], wd[:, cols], preferred_element_type=jnp.float32)
    out[...] = (part + arrived[...].astype(jnp.float32)).astype(jnp.bfloat16)


SMEM = pl.BlockSpec(memory_space=pltpu.SMEM)
VMEM = pl.BlockSpec(memory_space=pltpu.VMEM)
LIMIT = pltpu.CompilerParams(vmem_limit_bytes=32 * 1024 * 1024)


def hidden_of(order, xs, wg, wu, wd):
    rows, width = xs[0].shape
    hid = wg.shape[1]
    n = len(xs)
    return pl.pallas_call(
        hidden_kernel,
        in_specs=[SMEM] + [VMEM] * 7,
        out_specs=[VMEM] * 2,
        out_shape=[
            jax.ShapeDtypeStruct((rows, hid), jnp.bfloat16),
            jax.ShapeDtypeStruct((rows, width), jnp.bfloat16),
        ],
        compiler_params=LIMIT,
        cost_estimate=pl.CostEstimate(
            flops=2 * rows * width * hid * (2 * n + 1), bytes_accessed=6 * n * width * hid, transcendentals=rows * hid
        ),
    )(order, *xs, wg, wu, wd)


def down_of(j, order, hidden, arrived, wd):
    rows, hid = hidden.shape
    width = arrived.shape[1]
    return pl.pallas_call(
        lambda *refs: down_kernel(j, *refs),
        in_specs=[SMEM] + [VMEM] * 3,
        out_specs=VMEM,
        out_shape=jax.ShapeDtypeStruct((rows, width), jnp.bfloat16),
        compiler_params=LIMIT,
        cost_estimate=pl.CostEstimate(
            flops=2 * rows * width * hid, bytes_accessed=2 * width * hid + 4 * rows * width, transcendentals=0
        ),
    )(order, hidden, arrived, wd)


def ring_perm(groups, n):
    pairs = []
    for e in range(groups):
        for i in range(n):
            here, there = RING[i], RING[(i + (1 if e % 2 == 0 else -1)) % n]
            pairs.append((e * n + here, e * n + there))
    return pairs


def ring_layer(held, order, perm, wg, wu, wd):
    step = lambda a: lax.ppermute(a, ("expert", "blk"), perm)
    xs = [held]
    for _ in range(3):
        xs.append(step(xs[-1]))
    hidden, part = hidden_of(order, xs, wg, wu, wd)
    for j in (2, 3, 0):
        part = down_of(j, order, hidden, step(part), wd)
    return part


def square_program(tokens, route, gate_score, wg, wu, wd, capacity):
    groups, n = lax.axis_size("expert"), lax.axis_size("blk")
    me, place = lax.axis_index("expert"), lax.axis_index("blk")
    target = route[:, 0]
    relative = target ^ me
    slot_ids = relative * capacity + rank_of(target)
    selector = selector_of(slot_ids, groups * capacity)
    outgoing = jnp.dot(selector, tokens, preferred_element_type=jnp.float32).astype(jnp.bfloat16)
    chunks, width = groups // 2, tokens.shape[1]
    outgoing = outgoing.reshape(chunks, 2, capacity, width)
    sibling = lambda a: lax.ppermute(a, "expert", [(i, i ^ 1) for i in range(groups)])
    other = lambda a, k: lax.ppermute(a, "expert", [(i, i ^ (2 * k)) for i in range(groups)]) if k else a
    swapped = sibling(outgoing[:, 1])
    perm = ring_perm(groups, n)
    forward = {RING[i]: [RING[(i - s) % n] for s in range(n)] for i in range(n)}
    backward = {RING[i]: [RING[(i + s) % n] for s in range(n)] for i in range(n)}
    table = jnp.array([[forward[i] for i in range(n)], [backward[i] for i in range(n)]], jnp.int32)
    order = table[me % 2, place]
    backs = [None] * chunks
    for k in range(chunks):
        chunk = jnp.concatenate([outgoing[k, 0], swapped[k]], 0)
        shares = ring_layer(other(chunk, k), order, perm, wg, wu, wd)
        backs[k] = other(shares, k).reshape(2, capacity, width)
    own = jnp.stack([b[0] for b in backs])
    theirs = sibling(jnp.stack([b[1] for b in backs]))
    back = jnp.stack([own, theirs], 1).reshape(groups * capacity, width)
    picked = lax.dot_general(selector, back, (((0,), (0,)), ((), ())), preferred_element_type=jnp.float32)
    return (picked * gate_score).astype(jnp.bfloat16)


def plain_program(tokens, route, gate_score, w_gate, w_up, w_down, capacity):
    groups = lax.axis_size("expert")
    target = route[:, 0]
    selector = selector_of(target * capacity + rank_of(target), groups * capacity)
    outgoing = jnp.dot(selector, tokens, preferred_element_type=jnp.float32).astype(jnp.bfloat16)
    arrived = lax.all_to_all(outgoing, "expert", split_axis=0, concat_axis=0, tiled=True)
    whole = lax.all_gather(arrived, "blk", axis=1, tiled=True)
    gate_acc = jnp.dot(whole, w_gate, preferred_element_type=jnp.float32)
    up_acc = jnp.dot(whole, w_up, preferred_element_type=jnp.float32)
    hidden = (jax.nn.silu(gate_acc) * up_acc).astype(jnp.bfloat16)
    partial_sum = jnp.dot(hidden, w_down, preferred_element_type=jnp.float32)
    shares = lax.psum_scatter(partial_sum.astype(jnp.bfloat16), "blk", scatter_dimension=1, tiled=True)
    back = lax.all_to_all(shares, "expert", split_axis=0, concat_axis=0, tiled=True)
    picked = lax.dot_general(selector, back, (((0,), (0,)), ((), ())), preferred_element_type=jnp.float32)
    return (picked * gate_score).astype(jnp.bfloat16)


def per_device(tokens, route, gate_score, w_gate, w_up, w_down):
    groups, n = lax.axis_size("expert"), lax.axis_size("blk")
    count, width = tokens.shape
    capacity = 3 * count // (2 * groups)
    square = n == len(RING) and groups & (groups - 1) == 0 and width % 128 == 0 and capacity % 16 == 0
    program = square_program if square else plain_program
    return program(tokens, route, gate_score, w_gate[0], w_up[0], w_down[0], capacity)


def solution(mesh):
    in_specs = (
        P("expert", "blk"),
        P("expert", None),
        P("expert", None),
        P("expert", None, "blk"),
        P("expert", None, "blk"),
        P("expert", "blk", None),
    )
    return jax.shard_map(
        per_device, mesh=mesh, in_specs=in_specs, out_specs=P("expert", "blk"), check_vma=False
    )
```

```python
import jax
import jax.numpy as jnp
from jax import lax
from jax.experimental import pallas as pl
from jax.experimental.pallas import tpu as pltpu
from jax.sharding import PartitionSpec as P

RING = (0, 1, 3, 2)


def rank_of(target):
    count = target.shape[0]
    later = lax.broadcasted_iota(jnp.int32, (count, count), 0)
    before = lax.broadcasted_iota(jnp.int32, (count, count), 1) < later
    same = target[:, None] == target[None, :]
    return jnp.sum(jnp.where(same & before, 1, 0), axis=1).astype(jnp.int32)


def selector_of(slot_ids, slots):
    positions = lax.broadcasted_iota(jnp.int32, (slots, slot_ids.shape[0]), 0)
    return (positions == slot_ids[None, :]).astype(jnp.bfloat16)


def hidden_kernel(order, x0, x1, x2, x3, wg, wu, wd, hidden, part):
    width = x0.shape[1]
    gate = up = None
    for j, x in enumerate((x0, x1, x2, x3)):
        rows = pl.ds(pl.multiple_of(order[j] * width, width), width)
        g = jnp.dot(x[...], wg[rows, :], preferred_element_type=jnp.float32)
        u = jnp.dot(x[...], wu[rows, :], preferred_element_type=jnp.float32)
        gate, up = (g, u) if gate is None else (gate + g, up + u)
    hidden[...] = (gate / (1.0 + jnp.exp(-gate)) * up).astype(jnp.bfloat16)
    cols = pl.ds(pl.multiple_of(order[1] * width, width), width)
    part[...] = jnp.dot(hidden[...], wd[:, cols], preferred_element_type=jnp.float32).astype(jnp.bfloat16)


def down_kernel(j, order, hidden, arrived, wd, out):
    width = out.shape[1]
    cols = pl.ds(pl.multiple_of(order[j] * width, width), width)
    part = jnp.dot(hidden[...], wd[:, cols], preferred_element_type=jnp.float32)
    out[...] = (part + arrived[...].astype(jnp.float32)).astype(jnp.bfloat16)


SMEM = pl.BlockSpec(memory_space=pltpu.SMEM)
VMEM = pl.BlockSpec(memory_space=pltpu.VMEM)
COST = pl.CostEstimate(flops=1, bytes_accessed=1, transcendentals=0)
LIMIT = pltpu.CompilerParams(vmem_limit_bytes=12 * 1024 * 1024)


def order_kernel(order, wg, wu, wd, out):
    for j in range(order.shape[0]):
        out[j] = order[j]


def order_of(order, wg, wu, wd):
    return pl.pallas_call(
        order_kernel,
        in_specs=[SMEM] + [VMEM] * 3,
        out_specs=SMEM,
        out_shape=jax.ShapeDtypeStruct(order.shape, order.dtype),
        compiler_params=LIMIT,
        cost_estimate=COST,
    )(order, wg, wu, wd)


def hidden_of(order, xs, wg, wu, wd):
    rows, width = xs[0].shape
    hid = wg.shape[1]
    n = len(xs)
    return pl.pallas_call(
        hidden_kernel,
        in_specs=[SMEM] + [VMEM] * 7,
        out_specs=[VMEM] * 2,
        out_shape=[
            jax.ShapeDtypeStruct((rows, hid), jnp.bfloat16),
            jax.ShapeDtypeStruct((rows, width), jnp.bfloat16),
        ],
        compiler_params=LIMIT,
        cost_estimate=COST,
    )(order, *xs, wg, wu, wd)


def down_of(j, order, hidden, arrived, wd):
    rows, hid = hidden.shape
    width = arrived.shape[1]
    return pl.pallas_call(
        lambda *refs: down_kernel(j, *refs),
        in_specs=[SMEM] + [VMEM] * 3,
        out_specs=VMEM,
        out_shape=jax.ShapeDtypeStruct((rows, width), jnp.bfloat16),
        compiler_params=LIMIT,
        cost_estimate=COST,
    )(order, hidden, arrived, wd)


def ring_perm(groups, n):
    pairs = []
    for e in range(groups):
        for i in range(n):
            here, there = RING[i], RING[(i + (1 if e % 2 == 0 else -1)) % n]
            pairs.append((e * n + here, e * n + there))
    return pairs


def after(value, *done):
    return lax.optimization_barrier((value, *done))[0]


def turns_of(chunks):
    return TURNS if chunks == 4 else [k for _ in range(9) for k in range(chunks)]


TURNS = (1, 0, 1, 2, 0, 1, 2, 2, 1, 3, 2, 0, 1, 3, 2, 3, 2, 3, 2, 3, 1, 3, 2, 1, 3, 0, 0, 0, 3, 1, 2, 1, 0, 3)


def square_program(tokens, route, gate_score, wg, wu, wd, capacity):
    groups, n = lax.axis_size("expert"), lax.axis_size("blk")
    me, place = lax.axis_index("expert"), lax.axis_index("blk")
    target = route[:, 0]
    relative = target ^ me
    slot_ids = relative * capacity + rank_of(target)
    selector = selector_of(slot_ids, groups * capacity)
    outgoing = jnp.dot(selector, tokens, preferred_element_type=jnp.float32).astype(jnp.bfloat16)
    chunks, width = groups // 2, tokens.shape[1]
    outgoing = outgoing.reshape(chunks, 2, capacity, width)
    sibling = lambda a: lax.ppermute(a, "expert", [(i, i ^ 1) for i in range(groups)])
    other = lambda a, k: lax.ppermute(a, "expert", [(i, i ^ (2 * k)) for i in range(groups)])
    perm = ring_perm(groups, n)
    step = lambda a: lax.ppermute(a, ("expert", "blk"), perm)
    forward = {RING[i]: [RING[(i - s) % n] for s in range(n)] for i in range(n)}
    backward = {RING[i]: [RING[(i + s) % n] for s in range(n)] for i in range(n)}
    table = jnp.array([[forward[i] for i in range(n)], [backward[i] for i in range(n)]], jnp.int32)
    order = table[me % 2, place]

    swapped = sibling(outgoing[:, 1])
    packed = [jnp.concatenate([outgoing[k, 0], swapped[k]], 0) for k in range(chunks)]
    last = [order]
    pieces = {}

    def event(value):
        last[0] = after(value, last[0])
        return last[0]

    def chunk(k):
        held = packed[k]
        if k:
            held = other(held, k)
            yield
            held = event(held)
        xs = [held]
        for _ in range(n - 1):
            held = step(held)
            yield
            held = event(held)
            xs.append(held)
        hidden, part = hidden_of(order, xs, wg, wu, wd)
        for j in (*range(2, n), 0):
            part = step(part)
            yield
            part = down_of(j, order, hidden, event(part), wd)
            last[0] = part
        if k:
            part = other(part, k)
            yield
            part = event(part)
        theirs = sibling(part[capacity:])
        yield
        pieces[k] = [part[:capacity], event(theirs)]

    ways = [chunk(k) for k in range(chunks)]
    for k in range(chunks):
        next(ways[k])
    for turn, k in enumerate(turns_of(chunks)):
        with jax.named_scope("chunk%d" % k):
            next(ways[k], None)
        if turn == 1:
            order = last[0] = order_of(after(order, last[0]), wg, wu, wd)
    assert len(pieces) == chunks
    back = jnp.concatenate([piece for k in range(chunks) for piece in pieces[k]], 0)
    picked = lax.dot_general(selector, back, (((0,), (0,)), ((), ())), preferred_element_type=jnp.float32)
    return (picked * gate_score).astype(jnp.bfloat16)


def plain_program(tokens, route, gate_score, w_gate, w_up, w_down, capacity):
    groups = lax.axis_size("expert")
    target = route[:, 0]
    selector = selector_of(target * capacity + rank_of(target), groups * capacity)
    outgoing = jnp.dot(selector, tokens, preferred_element_type=jnp.float32).astype(jnp.bfloat16)
    arrived = lax.all_to_all(outgoing, "expert", split_axis=0, concat_axis=0, tiled=True)
    whole = lax.all_gather(arrived, "blk", axis=1, tiled=True)
    gate_acc = jnp.dot(whole, w_gate, preferred_element_type=jnp.float32)
    up_acc = jnp.dot(whole, w_up, preferred_element_type=jnp.float32)
    hidden = (jax.nn.silu(gate_acc) * up_acc).astype(jnp.bfloat16)
    partial_sum = jnp.dot(hidden, w_down, preferred_element_type=jnp.float32)
    shares = lax.psum_scatter(partial_sum.astype(jnp.bfloat16), "blk", scatter_dimension=1, tiled=True)
    back = lax.all_to_all(shares, "expert", split_axis=0, concat_axis=0, tiled=True)
    picked = lax.dot_general(selector, back, (((0,), (0,)), ((), ())), preferred_element_type=jnp.float32)
    return (picked * gate_score).astype(jnp.bfloat16)


def per_device(tokens, route, gate_score, w_gate, w_up, w_down):
    groups, n = lax.axis_size("expert"), lax.axis_size("blk")
    count, width = tokens.shape
    capacity = 3 * count // (2 * groups)
    square = n == len(RING) and groups & (groups - 1) == 0 and width % 128 == 0 and capacity % 16 == 0
    program = square_program if square else plain_program
    return program(tokens, route, gate_score, w_gate[0], w_up[0], w_down[0], capacity)


def solution(mesh):
    in_specs = (
        P("expert", "blk"),
        P("expert", None),
        P("expert", None),
        P("expert", None, "blk"),
        P("expert", None, "blk"),
        P("expert", "blk", None),
    )
    return jax.shard_map(
        per_device, mesh=mesh, in_specs=in_specs, out_specs=P("expert", "blk"), check_vma=False
    )
```

```python
import jax
import jax.numpy as jnp
from jax import lax
from jax.experimental import pallas as pl
from jax.experimental.pallas import tpu as pltpu
from jax.sharding import PartitionSpec as P

RING = (0, 1, 3, 2)


def rank_of(target):
    count = target.shape[0]
    later = lax.broadcasted_iota(jnp.int32, (count, count), 0)
    before = lax.broadcasted_iota(jnp.int32, (count, count), 1) < later
    same = target[:, None] == target[None, :]
    return jnp.sum(jnp.where(same & before, 1, 0), axis=1).astype(jnp.int32)


def selector_of(slot_ids, slots):
    positions = lax.broadcasted_iota(jnp.int32, (slots, slot_ids.shape[0]), 0)
    return (positions == slot_ids[None, :]).astype(jnp.bfloat16)


def hidden_kernel(order, x0, x1, x2, x3, wg, wu, wd, hidden, part):
    width = x0.shape[1]
    gate = up = None
    for j, x in enumerate((x0, x1, x2, x3)):
        rows = pl.ds(pl.multiple_of(order[j] * width, width), width)
        g = jnp.dot(x[...], wg[rows, :], preferred_element_type=jnp.float32)
        u = jnp.dot(x[...], wu[rows, :], preferred_element_type=jnp.float32)
        gate, up = (g, u) if gate is None else (gate + g, up + u)
    hidden[...] = (gate / (1.0 + jnp.exp(-gate)) * up).astype(jnp.bfloat16)
    cols = pl.ds(pl.multiple_of(order[1] * width, width), width)
    part[...] = jnp.dot(hidden[...], wd[:, cols], preferred_element_type=jnp.float32).astype(jnp.bfloat16)


def down_kernel(j, order, hidden, arrived, wd, out):
    width = out.shape[1]
    cols = pl.ds(pl.multiple_of(order[j] * width, width), width)
    part = jnp.dot(hidden[...], wd[:, cols], preferred_element_type=jnp.float32)
    out[...] = (part + arrived[...].astype(jnp.float32)).astype(jnp.bfloat16)


SMEM = pl.BlockSpec(memory_space=pltpu.SMEM)
VMEM = pl.BlockSpec(memory_space=pltpu.VMEM)
HBM = pl.BlockSpec(memory_space=pltpu.HBM)
COST = pl.CostEstimate(flops=1, bytes_accessed=1, transcendentals=0)
LONG = pl.CostEstimate(flops=10**11, bytes_accessed=1, transcendentals=0)
LIMIT = pltpu.CompilerParams(vmem_limit_bytes=12 * 1024 * 1024)


def across(row, lanes):
    return jnp.broadcast_to(row, (lanes, row.shape[1])).T


def dispatch_kernel(capacity, at, route, tokens, even, odd, ids, order):
    me, place = at[0], at[1]
    for j in range(order.shape[0]):
        way = jnp.where(me & 1 == 0, -j, j)
        number = ((place ^ (place >> 1)) + way) & (order.shape[0] - 1)
        order[j] = number ^ (number >> 1)
    count = tokens.shape[0]
    groups = 2 * even.shape[0] // capacity
    row = route[...]
    column = across(row.astype(jnp.float32), 128)[:, :1].astype(jnp.int32)
    first = lax.broadcasted_iota(jnp.int32, (count, count), 0)
    second = lax.broadcasted_iota(jnp.int32, (count, count), 1)
    earlier = jnp.where((column == row) & (first < second), 1.0, 0.0)
    rank = jnp.sum(earlier, axis=0, keepdims=True).astype(jnp.int32)
    relative = row ^ me
    own = ((relative & 1) * (groups // 2) + (relative >> 1)) * capacity + rank
    ids[...] = own
    slots = lax.broadcasted_iota(jnp.int32, (groups * capacity, count), 0)
    selector = jnp.where(slots == own, 1.0, 0.0).astype(jnp.bfloat16)
    rows = jnp.dot(selector, tokens[...], preferred_element_type=jnp.float32).astype(jnp.bfloat16)
    even[...] = rows[: even.shape[0]]
    odd[...] = rows[even.shape[0] :]


def dispatch(me, place, route, tokens, groups, capacity):
    count, width = tokens.shape
    half = jax.ShapeDtypeStruct((groups * capacity // 2, width), tokens.dtype)
    return pl.pallas_call(
        lambda *refs: dispatch_kernel(capacity, *refs),
        in_specs=[SMEM, VMEM, VMEM],
        out_specs=[VMEM] * 3 + [SMEM],
        out_shape=[
            half,
            half,
            jax.ShapeDtypeStruct((1, count), jnp.int32),
            jax.ShapeDtypeStruct((len(RING),), jnp.int32),
        ],
        compiler_params=LIMIT,
        cost_estimate=LONG,
    )(jnp.stack([me, place]), route.reshape(1, count), tokens)


def combine_kernel(ids, score, *refs):
    *pieces, out, rows = refs
    count, capacity = out.shape[0], pieces[-1].shape[0]
    half = len(pieces) // 2
    for k in range(half):
        rows[k * capacity : (k + 1) * capacity] = pieces[k][:capacity]
        rows[(half + k) * capacity : (half + k + 1) * capacity] = pieces[half + k][...]
    column = across(ids[...].astype(jnp.float32), 128)[:, :1].astype(jnp.int32)
    slots = lax.broadcasted_iota(jnp.int32, (count, rows.shape[0]), 1)
    selector = jnp.where(slots == column, 1.0, 0.0).astype(jnp.bfloat16)
    picked = jnp.dot(selector, rows[...], preferred_element_type=jnp.float32)
    out[...] = (picked * across(score[...], 128)[:, :1]).astype(jnp.bfloat16)


def combine(ids, score, mine, theirs):
    count, (capacity, width) = ids.shape[1], theirs[0].shape
    return pl.pallas_call(
        combine_kernel,
        in_specs=[VMEM] * (2 + 2 * len(mine)),
        out_specs=VMEM,
        out_shape=jax.ShapeDtypeStruct((count, width), jnp.bfloat16),
        scratch_shapes=[pltpu.VMEM((2 * len(mine) * capacity, width), jnp.bfloat16)],
        compiler_params=LIMIT,
        cost_estimate=COST,
    )(ids, score.reshape(1, count), *mine, *theirs)


def load_kernel(order, wg, wu, wd, order_out, wg_out, wu_out, wd_out, done):
    copies = [
        pltpu.make_async_copy(source, target, done.at[i])
        for i, (source, target) in enumerate(((wg, wg_out), (wu, wu_out), (wd, wd_out)))
    ]
    for copy in copies:
        copy.start()
    for j in range(order.shape[0]):
        order_out[j] = order[j]
    for copy in copies:
        copy.wait()


def load(order, *weights):
    return pl.pallas_call(
        load_kernel,
        in_specs=[SMEM] + [HBM] * 3,
        out_specs=[SMEM] + [VMEM] * 3,
        out_shape=[jax.ShapeDtypeStruct(a.shape, a.dtype) for a in (order, *weights)],
        scratch_shapes=[pltpu.SemaphoreType.DMA((3,))],
        compiler_params=LIMIT,
        cost_estimate=COST,
    )(order, *weights)


def hidden_of(order, xs, wg, wu, wd):
    rows, width = xs[0].shape
    hid = wg.shape[1]
    n = len(xs)
    return pl.pallas_call(
        hidden_kernel,
        in_specs=[SMEM] + [VMEM] * 7,
        out_specs=[VMEM] * 2,
        out_shape=[
            jax.ShapeDtypeStruct((rows, hid), jnp.bfloat16),
            jax.ShapeDtypeStruct((rows, width), jnp.bfloat16),
        ],
        compiler_params=LIMIT,
        cost_estimate=COST,
    )(order, *xs, wg, wu, wd)


def down_of(j, order, hidden, arrived, wd):
    rows, hid = hidden.shape
    width = arrived.shape[1]
    return pl.pallas_call(
        lambda *refs: down_kernel(j, *refs),
        in_specs=[SMEM] + [VMEM] * 3,
        out_specs=VMEM,
        out_shape=jax.ShapeDtypeStruct((rows, width), jnp.bfloat16),
        compiler_params=LIMIT,
        cost_estimate=COST,
    )(order, hidden, arrived, wd)


def ring_perm(groups, n):
    pairs = []
    for e in range(groups):
        for i in range(n):
            here, there = RING[i], RING[(i + (1 if e % 2 == 0 else -1)) % n]
            pairs.append((e * n + here, e * n + there))
    return pairs


def after(value, *done):
    return lax.optimization_barrier((value, *done))[0]


TURNS = (0, 3, 0, 1, 3, 3, 1, 2, 0, 3, 1, 2, 1, 2, 0, 3, 2, 1, 3, 2, 1, 3, 2, 1, 0, 3, 2, 1, 0, 0, 2, 0, 1, 3, 2)

HALVES = ()
LOAD_AT = 3


def turns_of(chunks):
    return TURNS if chunks == 4 else [k for _ in range(9) for k in range(chunks)]


def square_program(tokens, route, gate_score, wg, wu, wd, capacity):
    groups, n = lax.axis_size("expert"), lax.axis_size("blk")
    me, place = lax.axis_index("expert"), lax.axis_index("blk")
    chunks, width = groups // 2, tokens.shape[1]
    sibling = lambda a: lax.ppermute(a, "expert", [(i, i ^ 1) for i in range(groups)])
    other = lambda a, k: lax.ppermute(a, "expert", [(i, i ^ (2 * k)) for i in range(groups)])
    perm = ring_perm(groups, n)
    step = lambda a: lax.ppermute(a, ("expert", "blk"), perm)
    even, odd, ids, order = dispatch(me, place, route, tokens, groups, capacity)
    swapped = sibling(odd)
    part_of = lambda a, k: a[k * capacity : (k + 1) * capacity]
    packed = [jnp.concatenate([part_of(even, k), part_of(swapped, k)], 0) for k in range(chunks)]
    last = [order]
    mine, theirs, gathered = {}, {}, {}

    def event(value):
        last[0] = after(value, last[0])
        return last[0]

    def gather(name, held):
        xs = [held]
        for _ in range(n - 1):
            held = step(held)
            yield
            held = event(held)
            xs.append(held)
        gathered[name] = xs

    def arrive(k):
        held = other(packed[k], k)
        yield
        gathered[k] = [event(held)]

    def layer(k):
        hidden, part = hidden_of(order, gathered[k], wg, wu, wd)
        last[0] = part
        for j in (*range(2, n), 0):
            part = step(part)
            yield
            part = down_of(j, order, hidden, event(part), wd)
            last[0] = part
        if k:
            part = other(part, k)
            yield
            part = event(part)
        mine[k] = part
        back = sibling(part[capacity:])
        yield
        theirs[k] = event(back)

    def whole(k):
        if k:
            yield from arrive(k)
            yield from gather(k, gathered[k][0])
        else:
            yield from gather(k, packed[k])
            yield
        yield from layer(k)

    def first_of_halves(k):
        if k:
            yield from arrive(k)
            ways[chunks + 2 * k] = gather((k, 0), gathered[k][0][:capacity])
            ways[chunks + 2 * k + 1] = gather((k, 1), gathered[k][0][capacity:])
        else:
            ways[chunks] = gather((0, 0), part_of(even, 0))
            ways[chunks + 1] = gather((0, 1), part_of(swapped, 0))
        next(ways[chunks + 2 * k])
        next(ways[chunks + 2 * k + 1])
        yield
        gathered[k] = [jnp.concatenate(pair, 0) for pair in zip(gathered[k, 0], gathered[k, 1])]
        yield from layer(k)

    ways = {k: first_of_halves(k) if k in HALVES else whole(k) for k in range(chunks)}
    for k in range(chunks):
        next(ways[k])
    for turn, k in enumerate(turns_of(chunks)):
        if turn == LOAD_AT:
            order, wg, wu, wd = load(after(order, last[0]), wg, wu, wd)
            last[0] = order
        with jax.named_scope("chunk%d" % k):
            next(ways[k], None)
    return combine(ids, gate_score, [mine[k] for k in range(chunks)], [theirs[k] for k in range(chunks)])


def plain_program(tokens, route, gate_score, w_gate, w_up, w_down, capacity):
    groups = lax.axis_size("expert")
    target = route[:, 0]
    selector = selector_of(target * capacity + rank_of(target), groups * capacity)
    outgoing = jnp.dot(selector, tokens, preferred_element_type=jnp.float32).astype(jnp.bfloat16)
    arrived = lax.all_to_all(outgoing, "expert", split_axis=0, concat_axis=0, tiled=True)
    whole = lax.all_gather(arrived, "blk", axis=1, tiled=True)
    gate_acc = jnp.dot(whole, w_gate, preferred_element_type=jnp.float32)
    up_acc = jnp.dot(whole, w_up, preferred_element_type=jnp.float32)
    hidden = (jax.nn.silu(gate_acc) * up_acc).astype(jnp.bfloat16)
    partial_sum = jnp.dot(hidden, w_down, preferred_element_type=jnp.float32)
    shares = lax.psum_scatter(partial_sum.astype(jnp.bfloat16), "blk", scatter_dimension=1, tiled=True)
    back = lax.all_to_all(shares, "expert", split_axis=0, concat_axis=0, tiled=True)
    picked = lax.dot_general(selector, back, (((0,), (0,)), ((), ())), preferred_element_type=jnp.float32)
    return (picked * gate_score).astype(jnp.bfloat16)


def per_device(tokens, route, gate_score, w_gate, w_up, w_down):
    groups, n = lax.axis_size("expert"), lax.axis_size("blk")
    count, width = tokens.shape
    capacity = 3 * count // (2 * groups)
    square = n == len(RING) and groups & (groups - 1) == 0 and width % 128 == 0 and capacity % 16 == 0
    program = square_program if square else plain_program
    return program(tokens, route, gate_score, w_gate[0], w_up[0], w_down[0], capacity)


def solution(mesh):
    in_specs = (
        P("expert", "blk"),
        P("expert", None),
        P("expert", None),
        P("expert", None, "blk"),
        P("expert", None, "blk"),
        P("expert", "blk", None),
    )
    return jax.shard_map(
        per_device, mesh=mesh, in_specs=in_specs, out_specs=P("expert", "blk"), check_vma=False
    )
```
